32 devices in a mesh: tm: 8 (over y, x, core), space: 4 (over z).
Axes of the slice: x: 2, y: 2, z: 4, core: 2. Of those that a mesh axis runs over, the one named last changes fastest.
Arguments:
- opening_guess_profile: float32 [8, 16, 128, 256], P('tm', 'space'), may hold values from -6 to 6
- capacity: float32 [16, 128, 256], P('space'), may hold values from 0.25 to 4
- thermal_forcing: float32 [8, 16, 128, 256], P('tm', 'space'), may hold values from -3 to 3
- rough_decay_factor: float32 [8, 16, 128, 256], P('tm', 'space'), may hold values from 0.2 to 1
- tile_ids: int32 [64, 32], P('tm', 'space'), may hold values from 0 to 2047, as said below
- tile_count: int32 [64, 4], P('tm', 'space'), may hold values from 2 to 8, as said below
- tile_blocks: float32 [64, 32, 64, 64], P('tm', 'space'), may hold values from -0.25 to 0.25
Outputs:
- updated_opening_state: float32 [8, 16, 128, 256], P('tm', 'space')
- accurate_ending_thermal_state: float32 [8, 16, 128, 256], P('tm', 'space')
The draws below stay inside these ranges and needn't reach their ends.
Inputs may be any that keep to these rules, and one draw needn't show every extreme that they name: `tile_ids`: the 8 entries of one brick for one step are distinct tile numbers of that brick. `tile_count`: on every brick of every slab some step uses all 8 slots.
All inputs are finite; a program needn't handle non-finite values.
Results may differ from the reference program's by a relative error of at most 0.0003.
Values sent between devices are 32-bit elements; how exact they have to be, the bound alone decides.
No kernel may reach another device: no remote copies, remote signals or barrier semaphores. Data moves between devices by JAX's collectives and lax.ppermute only.
A program may use at most 128 MiB of HBM per device.

```python
import math
import jax
import jax.numpy as jnp
from jax import lax

NY = 128
NZ = 256
INCREMENTS = 8
SWEEPS = 4
TILE = 64
MAXT = 8
NX = 16
TILES_DEV = 2048
N_TM = 8
N_SPACE = 4


def draw_rough_decay_factor(key, part):
    key_one, random_key_second, random_key_third = jax.random.split(key, 3)
    shape = (N_TM, NX, NY, NZ)
    exponent = jax.random.uniform(key_one, shape, jnp.float32, -3.0, -0.3)
    rough_estimate = 1.0 - jnp.power(10.0, exponent)
    slab_groups_total = jax.random.randint(random_key_second, (3,), 0, N_TM)
    hit_marker = jnp.any(jnp.arange(N_TM)[:, None] == slab_groups_total[None, :], axis=1)
    factor = jax.random.uniform(random_key_third, shape, jnp.float32, 0.5, 0.8)
    rough_estimate = jnp.where(hit_marker[:, None, None, None], rough_estimate * factor, rough_estimate)
    return rough_estimate.astype(jnp.float32)


def draw_tile_ids(key, part):
    scores = jax.random.randint(key, (N_TM * INCREMENTS, N_SPACE, TILES_DEV), 0, 2 ** 18)
    scores = scores * TILES_DEV + jnp.arange(TILES_DEV, dtype=jnp.int32)
    unused_value, chosen = lax.top_k(scores, MAXT)
    return chosen.reshape(N_TM * INCREMENTS, N_SPACE * MAXT).astype(jnp.int32)


def draw_tile_count(key, part):
    key_one, random_key_second = jax.random.split(key)
    counts = jax.random.randint(key_one, (N_TM, INCREMENTS, N_SPACE), MAXT // 4, MAXT + 1)
    full_step = jax.random.randint(random_key_second, (N_TM, 1, N_SPACE), 0, INCREMENTS)
    counts = jnp.where(jnp.arange(INCREMENTS)[None, :, None] == full_step, MAXT, counts)
    return counts.reshape(N_TM * INCREMENTS, N_SPACE).astype(jnp.int32)


def block_scale(key, dims, pieces, low, high):
    factor_of = 1.0
    for axis_at, parts in pieces:
        heights = jax.random.uniform(jax.random.fold_in(jax.random.fold_in(key, 6), axis_at), (parts,), jnp.float32, low / len(pieces), high / len(pieces))
        factor_of = factor_of * jnp.repeat(jnp.exp(heights), dims[axis_at] // parts).reshape((-1,) + (1,) * (len(dims) - 1 - axis_at))
    return factor_of


def gaussian(stream_key, shape, deviation, most, pieces=(), kind=jnp.bfloat16):
    factor_of = block_scale(stream_key, shape, pieces, -0.22, 0.18) if pieces else 1.0
    array = jax.random.normal(stream_key, shape, jnp.float32) * deviation * factor_of
    return jnp.minimum(jnp.maximum(array, -most), most).astype(kind)


def setup_inputs(seed: int = 0) -> dict:
    arg_keys = jax.random.split(jax.random.key(seed), 8)
    return {
        "opening_guess_profile": gaussian(arg_keys[0], (N_TM, NX, NY, NZ), 1.0, 6.0, ((0, 8), (1, 4)), jnp.float32),
        "capacity": jnp.clip(jnp.exp(math.log(4.0) - 2.7725887 * jax.random.uniform(arg_keys[1], (NX, NY, NZ), jnp.float32) ** block_scale(arg_keys[1], (NX, NY, NZ), ((0, 4),), -0.2, 0.2)), 0.25, 4.0),
        "thermal_forcing": gaussian(arg_keys[2], (N_TM, NX, NY, NZ), 0.5, 3.0, ((0, 8), (1, 4)), jnp.float32),
        "rough_decay_factor": draw_rough_decay_factor(jax.random.fold_in(arg_keys[7], 71), 0),
        "tile_ids": draw_tile_ids(jax.random.fold_in(arg_keys[7], 71), 0),
        "tile_count": draw_tile_count(jax.random.fold_in(arg_keys[7], 71), 0),
        "tile_blocks": gaussian(arg_keys[6], (N_TM * INCREMENTS, N_SPACE * MAXT, TILE, TILE), 512 ** -0.5, 0.25, ((0, 8), (1, 4)), jnp.float32),
    }


COND = 1.0


def beside_sum(wide):
    center = wide[1:-1]
    padded = jnp.pad(center, ((0, 0), (1, 1), (1, 1)))
    total = wide[2:] + wide[:-2]
    total = total + padded[:, 2:, 1:-1] + padded[:, :-2, 1:-1]
    return total + padded[:, 1:-1, 2:] + padded[:, 1:-1, :-2]


def interface_fix(field, previous, tile_rows, live_count, blocks):
    shape = field.shape
    tile_len = blocks.shape[-1]
    delta = (field - previous).reshape(-1, tile_len)
    picked = delta[tile_rows]
    fixes = jnp.einsum("src,sc->sr", blocks, picked, precision=lax.Precision.HIGHEST)
    live = (jnp.arange(tile_rows.shape[0]) < live_count)[:, None]
    fixes = jnp.where(live, fixes, 0.0)
    tiles = field.reshape(-1, tile_len).at[tile_rows].add(fixes)
    return tiles.reshape(shape)


def slab_run(args):
    opening_moment, source, capacity, window_labels, window_tallies, window_partitions = args
    inverse = 1.0 / (capacity + 6.0 * COND)
    field = opening_moment
    for step_index in range(INCREMENTS):
        previous = field
        rhs = capacity * previous + source
        for sweep_index in range(SWEEPS):
            wide = jnp.pad(field, ((1, 1), (0, 0), (0, 0)))
            field = (rhs + COND * beside_sum(wide)) * inverse
        bricks = field.reshape(N_SPACE, -1, NY, NZ)
        old_bricks = previous.reshape(N_SPACE, -1, NY, NZ)
        rows = window_labels[step_index].reshape(N_SPACE, MAXT)
        counts = window_tallies[step_index]
        blocks = window_partitions[step_index].reshape(N_SPACE, MAXT, TILE, TILE)
        bricks = jax.vmap(interface_fix)(bricks, old_bricks, rows, counts, blocks)
        field = bricks.reshape(field.shape)
    return field


def reference(opening_guess_profile, capacity, thermal_forcing, rough_decay_factor, tile_ids, tile_count, tile_blocks):
    window_labels = tile_ids.reshape(N_TM, INCREMENTS, -1)
    window_tallies = tile_count.reshape(N_TM, INCREMENTS, -1)
    window_partitions = tile_blocks.reshape(N_TM, INCREMENTS, -1, TILE, TILE)

    def lone_window(args):
        opening_moment, source, slab_id, slab_count, slab_block = args
        return slab_run((opening_moment, source, capacity, slab_id, slab_count, slab_block))

    accurate_ending_thermal_state = lax.map(lone_window, (opening_guess_profile, thermal_forcing, window_labels, window_tallies, window_partitions))

    def propagation_sequence(carry, items):
        index, opening_moment, ending, rough_estimate = items
        first = index == 0
        current = jnp.where(first, opening_moment, carry)
        following = jnp.where(first, ending, rough_estimate * (carry - opening_moment) + ending)
        return following, current

    position_numbers = jnp.arange(N_TM).astype(jnp.int32)
    unused_value, updated_opening_state = lax.scan(propagation_sequence, jnp.zeros_like(opening_guess_profile[0]), (position_numbers, opening_guess_profile, accurate_ending_thermal_state, rough_decay_factor))
    return updated_opening_state, accurate_ending_thermal_state
```

```python
import functools

import jax
import jax.numpy as jnp
from jax import lax
from jax.experimental import pallas as pl
from jax.experimental.pallas import tpu as pltpu
from jax.sharding import PartitionSpec as P

SWEEPS = 4
COND = 1.0
SUB = 8
LANE = 128
STAGES = 4


class Halves(list):
    def start(self):
        for copy in self:
            copy.start()

    def wait(self):
        for copy in self:
            copy.wait()


def steps_kernel(shape, slots, tile, first, with_pack, *refs):
    bricks, width, rows, depth = shape
    planes = bricks * width
    rung = rows // SUB
    half = depth // LANE
    count = bricks * slots
    place, lists = refs[0], refs[1]
    refs = refs[2:]
    if with_pack:
        packs, refs = refs[:bricks], refs[bricks:]
        states = [pack.at[0] for pack in packs]
    else:
        states, packs, refs = refs[:bricks], refs[bricks : 2 * bricks], refs[2 * bricks :]
    blocks, refs = refs[:bricks], refs[bricks:]
    outs, refs = refs[:bricks], refs[bricks:]
    stage, field, other, source, capacity, inverse, rhs, kept, picked, fixes, held, stage_sem, held_sem = refs
    steps = blocks[0].shape[0]
    all_steps = lists.shape[0] // (bricks * (slots + 1))

    def fetch_blocks(step, slot):
        return [
            pltpu.make_async_copy(blocks[i].at[step], held.at[slot, place[i]], held_sem.at[slot, i])
            for i in range(bricks)
        ]

    for copy in fetch_blocks(0, 0):
        copy.start()

    loads = []
    for i in range(bricks):
        loads.append((packs[i].at[2], capacity, i))
        loads.append((packs[i].at[1], source, i))
        loads.append((states[i], field, i))

    def halves(whole, n, inward):
        copies = Halves()
        for h in range(half):
            there, here = whole.at[:, :, pl.ds(h * LANE, LANE)], stage.at[n % STAGES, h]
            ends = (there, here) if inward else (here, there)
            copies.append(pltpu.make_async_copy(*ends, stage_sem.at[n % STAGES, h]))
        return copies

    def load_copy(n):
        return halves(loads[n][0], n, True)

    for n in range(min(STAGES, len(loads))):
        load_copy(n).start()
    zero = jnp.zeros((rung, SUB, depth), jnp.float32)
    for edge in (0, planes + 1):
        field[edge] = zero
        other[edge] = zero
    for n, (_, target, i) in enumerate(loads):
        load_copy(n).wait()
        offset = 1 if target is field else 0
        first_plane = place[i] * width + offset

        def spread(x, _, n=n, target=target, first_plane=first_plane):
            for r in range(rung):
                for h in range(half):
                    lanes = pl.ds(h * LANE, LANE)
                    value = stage[n % STAGES, h, x, pl.ds(r, SUB, stride=rung), :]
                    target[first_plane + x, r, :, lanes] = value
                    if target is capacity:
                        inverse[first_plane + x, r, :, lanes] = 1.0 / (value + 6.0 * COND)
            return 0

        lax.fori_loop(0, width, spread, 0)
        if n + STAGES < len(loads):
            load_copy(n + STAGES).start()

    lane = lax.broadcasted_iota(jnp.int32, (SUB, LANE), 1)
    low, high = lane == 0, lane == LANE - 1
    sub = lax.broadcasted_iota(jnp.int32, (SUB, LANE), 0)
    top, bottom = sub == 0, sub == SUB - 1

    def sweep(src, dst, opening):
        def plane(x, _):
            center = [[src[x + 1, r, :, pl.ds(h * LANE, LANE)] for h in range(half)] for r in range(rung)]
            for r in range(rung):
                row = center[r]
                lefts = [pltpu.roll(v, 1, 1) for v in row]
                rights = [pltpu.roll(v, LANE - 1, 1) for v in row]
                for h in range(half):
                    lanes = pl.ds(h * LANE, LANE)
                    left = jnp.where(low, lefts[h - 1] if h else 0.0, lefts[h])
                    right = jnp.where(high, rights[h + 1] if h + 1 < half else 0.0, rights[h])
                    if r:
                        above = center[r - 1][h]
                    else:
                        above = jnp.where(top, 0.0, pltpu.roll(center[rung - 1][h], 1, 0))
                    if r + 1 < rung:
                        below = center[r + 1][h]
                    else:
                        below = jnp.where(bottom, 0.0, pltpu.roll(center[0][h], SUB - 1, 0))
                    total = (src[x, r, :, lanes] + src[x + 2, r, :, lanes]) + (above + below) + (left + right)
                    if opening:
                        base = capacity[x, r, :, lanes] * row[h] + source[x, r, :, lanes]
                        rhs[x, r, :, lanes] = base
                    else:
                        base = rhs[x, r, :, lanes]
                    dst[x + 1, r, :, lanes] = (base + COND * total) * inverse[x, r, :, lanes]
            return 0

        lax.fori_loop(0, planes, plane, 0)

    quarter = lax.broadcasted_iota(jnp.int32, (1, depth), 1) // tile
    per_row = depth // tile
    tile_lane = lax.broadcasted_iota(jnp.int32, (1, LANE), 1)
    group = LANE // tile

    def cell_of(step, b, s):
        at = (b * all_steps + first + step) * (slots + 1)
        t = lists[at + s]
        live = s < lists[at + slots]
        line = t // per_row
        x, y = line // rows, line % rows
        part = jnp.where(live, t % per_row, -1)
        return b * width + x + 1, y % rung, y // rung, part

    def one_step(step, _):
        slot = step % 2

        @pl.when(step + 1 < steps)
        def _():
            for copy in fetch_blocks(step + 1, 1 - slot):
                copy.start()

        def keep(b, _):
            for s in range(slots):
                x, r, u, _unused = cell_of(step, b, s)
                kept[pl.ds(b * slots + s, 1), :] = field[x, r, pl.ds(u, 1), :]
            return 0

        lax.fori_loop(0, bricks, keep, 0)
        sweep(field, other, True)
        for _pair in range((SWEEPS - 2) // 2):
            sweep(other, field, False)
            sweep(field, other, False)
        sweep(other, field, False)

        def pick(b, _):
            for s in range(slots):
                x, r, u, part = cell_of(step, b, s)
                n = b * slots + s
                delta = field[x, r, pl.ds(u, 1), :] - kept[pl.ds(n, 1), :]
                delta = jnp.where(quarter == part, delta, 0.0)
                folded = delta[:, :LANE]
                for h in range(1, half):
                    folded = folded + delta[:, h * LANE : (h + 1) * LANE]
                whole = folded
                for g in range(1, group):
                    whole = whole + pltpu.roll(folded, g * tile, 1)
                picked[pl.ds(n, 1), :] = whole
            return 0

        lax.fori_loop(0, bricks, pick, 0)
        for copy in fetch_blocks(step, slot):
            copy.wait()

        def multiply(b, columns):
            for s in range(slots):
                n = b * slots + s
                products = held[slot, b, s] * picked[pl.ds(n, 1), :]
                parts = [
                    jnp.sum(jnp.where(tile_lane // tile == g, products, 0.0), axis=1, keepdims=True)
                    for g in range(group)
                ]
                column = jnp.concatenate(parts, axis=0)
                columns = jnp.where(tile_lane == n, column, columns)
            return columns

        columns = lax.fori_loop(0, bricks, multiply, jnp.zeros((tile, LANE), jnp.float32))
        fixes[...] = jnp.concatenate([columns] * group, axis=0).T

        def apply(b, _):
            for s in range(slots):
                x, r, u, part = cell_of(step, b, s)
                fix = fixes[pl.ds(b * slots + s, 1), :]
                fix = jnp.where(quarter == part, jnp.concatenate([fix] * half, axis=1), 0.0)
                field[x, r, pl.ds(u, 1), :] = field[x, r, pl.ds(u, 1), :] + fix
            return 0

        lax.fori_loop(0, bricks, apply, 0)
        return 0

    lax.fori_loop(0, steps, one_step, 0)

    def store_copy(i):
        return halves(outs[i], i, False)

    for i in range(bricks):
        if i >= STAGES:
            store_copy(i - STAGES).wait()
        first_plane = place[i] * width + 1

        def gather(x, _, i=i, first_plane=first_plane):
            for r in range(rung):
                for h in range(half):
                    lanes = pl.ds(h * LANE, LANE)
                    stage[i % STAGES, h, x, pl.ds(r, SUB, stride=rung), :] = field[first_plane + x, r, :, lanes]
            return 0

        lax.fori_loop(0, width, gather, 0)
        store_copy(i).start()
    for i in range(max(0, bricks - STAGES), bricks):
        store_copy(i).wait()


def run_steps(place, lists, states, packs, blocks, first, slots, tile):
    with_pack = states is None
    bricks = len(packs)
    _, width, rows, depth = packs[0].shape
    planes, rung = bricks * width, rows // SUB
    steps = blocks[0].shape[0]
    count = bricks * slots
    body = functools.partial(steps_kernel, (bricks, width, rows, depth), slots, tile, first, with_pack)
    smem = pl.BlockSpec(memory_space=pltpu.SMEM)
    hbm = pl.BlockSpec(memory_space=pl.ANY)
    operands = ([] if with_pack else list(states)) + list(packs) + list(blocks)
    grid_shape = (planes, rung, SUB, depth)
    wide_shape = (planes + 2, rung, SUB, depth)
    packed = blocks[0].shape[2:]
    cells = planes * rows * depth
    return pl.pallas_call(
        body,
        out_shape=[jax.ShapeDtypeStruct((width, rows, depth), jnp.float32)] * bricks,
        in_specs=[smem, smem] + [hbm] * len(operands),
        out_specs=[hbm] * bricks,
        scratch_shapes=[
            pltpu.VMEM((STAGES, depth // LANE, width, rows, LANE), jnp.float32),
            pltpu.VMEM(wide_shape, jnp.float32),
            pltpu.VMEM(wide_shape, jnp.float32),
            pltpu.VMEM(grid_shape, jnp.float32),
            pltpu.VMEM(grid_shape, jnp.float32),
            pltpu.VMEM(grid_shape, jnp.float32),
            pltpu.VMEM(grid_shape, jnp.float32),
            pltpu.VMEM((count, depth), jnp.float32),
            pltpu.VMEM((count, LANE), jnp.float32),
            pltpu.VMEM((LANE, LANE), jnp.float32),
            pltpu.VMEM((2, bricks, slots) + packed, jnp.float32),
            pltpu.SemaphoreType.DMA((STAGES, depth // LANE)),
            pltpu.SemaphoreType.DMA((2, bricks)),
        ],
        compiler_params=pltpu.CompilerParams(vmem_limit_bytes=60 * 1024 * 1024),
        cost_estimate=pl.CostEstimate(
            flops=cells * steps * SWEEPS * 10, bytes_accessed=cells * 4 * steps * 8, transcendentals=0
        ),
    )(place, lists, *operands)


def routes(windows, bricks):
    home = bricks // 2 - 1
    others = [z for z in range(bricks) if z != home]

    def at(t, z):
        return t * bricks + (z if t % 2 == 0 else bricks - 1 - z)

    rounds = [[(at(t, z), at(t, home)) for t in range(windows)] for z in others]
    return home, others, rounds


def shards(
    opening_guess_profile,
    capacity,
    thermal_forcing,
    rough_decay_factor,
    tile_ids,
    tile_count,
    tile_blocks,
):
    axes = ("tm", "space")
    windows, bricks = lax.axis_size("tm"), lax.axis_size("space")
    window, brick = lax.axis_index("tm"), lax.axis_index("space")
    opening = opening_guess_profile[0]
    rough = rough_decay_factor[0]
    width, rows, depth = opening.shape
    steps, slots = tile_ids.shape
    tile = tile_blocks.shape[-1]
    home, others, rounds = routes(windows, bricks)
    place = jnp.array([home] + others, jnp.int32)
    place = jnp.where(window % 2 == 0, place, bricks - 1 - place)

    lists = lax.all_gather(jnp.concatenate([tile_ids, tile_count], axis=1), "space").reshape(-1)
    pack = jnp.stack([opening, thermal_forcing[0], capacity])
    group = LANE // tile
    share = tile // group
    blocks = jnp.concatenate([tile_blocks[:, :, g * share : (g + 1) * share] for g in range(group)], axis=-1)
    early = steps // 2

    def spread(value):
        return [lax.ppermute(value, axes, pairs) for pairs in rounds]

    packs = spread(pack)
    blocks_early = spread(blocks[:early])
    states = run_steps(
        place, lists, None, [pack] + packs, [blocks[:early]] + blocks_early, 0, slots, tile
    )
    late, _ = lax.optimization_barrier((blocks[early:], packs[-1]))
    blocks_late = spread(late)
    states = run_steps(place, lists, states, [pack] + packs, [late] + blocks_late, early, slots, tile)

    held_here = brick == place[0]
    ending = jnp.where(held_here, states[0], 0.0)
    for pairs, state in zip(rounds, states[1:]):
        ending = ending + lax.ppermute(state, axes, [(b, a) for a, b in pairs])

    def swap(value):
        parts = value.reshape(windows, -1, depth)
        return lax.all_to_all(parts, "tm", 0, 0, tiled=True)

    factors = swap(rough)
    shift = jnp.where(window == 0, ending, ending - rough * opening)
    shifts = swap(shift)
    x = shifts[0]
    arrived = [x]
    for j in range(1, windows):
        arrived.append(x)
        x = factors[j] * x + shifts[j]
    result = swap(jnp.stack(arrived)).reshape(width, rows, depth)
    updated = jnp.where(window == 0, opening, result)
    return (updated[None], ending[None])


def solution(mesh):
    in_specs = (
        P("tm", "space", None, None),
        P("space", None, None),
        P("tm", "space", None, None),
        P("tm", "space", None, None),
        P("tm", "space"),
        P("tm", "space"),
        P("tm", "space", None, None),
    )
    out_specs = (P("tm", "space", None, None), P("tm", "space", None, None))
    return jax.shard_map(shards, mesh=mesh, in_specs=in_specs, out_specs=out_specs, check_vma=False)
```

```python
import functools

import jax
import jax.numpy as jnp
from jax import lax
from jax.experimental import pallas as pl
from jax.experimental.pallas import tpu as pltpu
from jax.sharding import PartitionSpec as P

SWEEPS = 4
COND = 1.0
SUB = 8
LANE = 128
EARLY = 3
SPAN = 8


def span_of(planes):
    return max(n for n in range(1, SPAN + 1) if planes % n == 0)


def steps_kernel(shape, slots, tile, first, with_pack, *refs):
    bricks, width, rung, depth = shape
    planes = bricks * width
    half = depth // LANE
    count = bricks * slots
    place, lists = refs[0], refs[1]
    refs = refs[2:]
    if with_pack:
        packs, refs = refs[:bricks], refs[bricks:]
        states = [pack.at[0] for pack in packs]
    else:
        states, packs, refs = refs[:bricks], refs[bricks : 2 * bricks], refs[2 * bricks :]
    blocks, refs = refs[:bricks], refs[bricks:]
    outs, refs = refs[:bricks], refs[bricks:]
    field, other, source, capacity, inverse, rhs, kept, current, picked, fixes, held, load_sem, held_sem = refs
    steps = blocks[0].shape[0]
    all_steps = lists.shape[0] // (count * 4)

    def fetch_blocks(step, slot):
        return [
            pltpu.make_async_copy(blocks[i].at[step], held.at[slot, place[i]], held_sem.at[slot, i])
            for i in range(bricks)
        ]

    loads = []
    for i in range(bricks):
        loads.append((packs[i].at[2], capacity.at[pl.ds(place[i] * width, width)]))
    for i in range(bricks):
        loads.append((states[i], field.at[pl.ds(place[i] * width + 1, width)]))
        loads.append((packs[i].at[1], source.at[pl.ds(place[i] * width, width)]))
    loads = [pltpu.make_async_copy(*ends, load_sem.at[n]) for n, ends in enumerate(loads)]
    for copy in loads:
        copy.start()
    for copy in fetch_blocks(0, 0):
        copy.start()

    zero = jnp.zeros((rung, SUB, depth), jnp.float32)
    for edge in (0, planes + 1):
        field[edge] = zero
        other[edge] = zero
    for copy in loads[:bricks]:
        copy.wait()

    def invert(x, _):
        inverse[x] = 1.0 / (capacity[x] + 6.0 * COND)
        return 0

    lax.fori_loop(0, planes, invert, 0)
    for copy in loads[bricks:]:
        copy.wait()

    sub = lax.broadcasted_iota(jnp.int32, (SUB, LANE), 0)
    top, bottom = sub == 0, sub == SUB - 1
    line = lax.broadcasted_iota(jnp.int32, (depth, depth), 0)
    column = lax.broadcasted_iota(jnp.int32, (depth, depth), 1)
    beside = jnp.where(jnp.abs(line - column) == 1, 1.0, 0.0).astype(jnp.bfloat16)
    span = span_of(planes)

    def split(value):
        coarse = value.astype(jnp.bfloat16)
        return coarse, (value - coarse.astype(jnp.float32)).astype(jnp.bfloat16)

    def product(value, matrix):
        coarse, fine = split(value)
        return jnp.dot(coarse, matrix, preferred_element_type=jnp.float32) + jnp.dot(
            fine, matrix, preferred_element_type=jnp.float32
        )

    def sweep(src, dst, opening):
        def chunk(n, _):
            whole = src[pl.ds(n * span + 1, span)].reshape(span * rung * SUB, depth)
            along = product(whole, beside).reshape(span, rung, SUB, depth)
            for p in range(span):
                x = n * span + p
                center = [[src[x + 1, r, :, pl.ds(h * LANE, LANE)] for h in range(half)] for r in range(rung)]
                for r in range(rung):
                    for h in range(half):
                        lanes = pl.ds(h * LANE, LANE)
                        if r:
                            above = center[r - 1][h]
                        else:
                            above = jnp.where(top, 0.0, pltpu.roll(center[rung - 1][h], 1, 0))
                        if r + 1 < rung:
                            below = center[r + 1][h]
                        else:
                            below = jnp.where(bottom, 0.0, pltpu.roll(center[0][h], SUB - 1, 0))
                        total = src[x, r, :, lanes] + src[x + 2, r, :, lanes]
                        total = total + (above + below) + along[p, r, :, h * LANE : (h + 1) * LANE]
                        if opening:
                            base = capacity[x, r, :, lanes] * center[r][h] + source[x, r, :, lanes]
                            rhs[x, r, :, lanes] = base
                        else:
                            base = rhs[x, r, :, lanes]
                        dst[x + 1, r, :, lanes] = (base + COND * total) * inverse[x, r, :, lanes]
            return 0

        lax.fori_loop(0, planes // span, chunk, 0)

    quarter = lax.broadcasted_iota(jnp.int32, (1, depth), 1) // tile
    group = LANE // tile
    share = tile // group
    from_lane = lax.broadcasted_iota(jnp.int32, (LANE, LANE), 0)
    to_lane = lax.broadcasted_iota(jnp.int32, (LANE, LANE), 1)
    gathers = jnp.where(from_lane // tile == (to_lane % tile) // share, 1.0, 0.0).astype(jnp.bfloat16)
    own_line = lax.broadcasted_iota(jnp.int32, (share, LANE), 0)
    own_lane = lax.broadcasted_iota(jnp.int32, (share, LANE), 1)
    diagonal = own_line == own_lane % share

    def cell_of(step, b, s):
        at = ((b * all_steps + first + step) * slots + s) * 4
        return lists[at], lists[at + 1], lists[at + 2], lists[at + 3]

    def one_step(step, _):
        slot = step % 2

        @pl.when(step + 1 < steps)
        def _():
            for copy in fetch_blocks(step + 1, 1 - slot):
                copy.start()

        def keep(b, _):
            for s in range(slots):
                x, r, u, _unused = cell_of(step, b, s)
                kept[pl.ds(b * slots + s, 1), :] = field[x, r, pl.ds(u, 1), :]
            return 0

        lax.fori_loop(0, bricks, keep, 0)
        sweep(field, other, True)
        for _pair in range((SWEEPS - 2) // 2):
            sweep(other, field, False)
            sweep(field, other, False)
        sweep(other, field, False)

        def pick(b, _):
            for s in range(slots):
                x, r, u, part = cell_of(step, b, s)
                n = b * slots + s
                value = field[x, r, pl.ds(u, 1), :]
                current[pl.ds(n, 1), :] = value
                delta = jnp.where(quarter == part, value - kept[pl.ds(n, 1), :], 0.0)
                folded = delta[:, :LANE]
                for h in range(1, half):
                    folded = folded + delta[:, h * LANE : (h + 1) * LANE]
                whole = folded
                for g in range(1, group):
                    whole = whole + pltpu.roll(folded, g * tile, 1)
                picked[pl.ds(n, 1), :] = whole
            return 0

        lax.fori_loop(0, bricks, pick, 0)
        for copy in fetch_blocks(step, slot):
            copy.wait()

        def multiply(b, _):
            terms = [held[slot, b, s] * picked[pl.ds(b * slots + s, 1), :] for s in range(slots)]
            sums = product(jnp.concatenate(terms, axis=0), gathers)
            for s in range(slots):
                fix = jnp.where(diagonal, sums[s * share : (s + 1) * share], 0.0)
                fixes[pl.ds(b * slots + s, 1), :] = jnp.sum(fix, axis=0, keepdims=True)
            return 0

        lax.fori_loop(0, bricks, multiply, 0)

        def apply(b, _):
            for s in range(slots):
                x, r, u, part = cell_of(step, b, s)
                n = b * slots + s
                fix = jnp.concatenate([fixes[pl.ds(n, 1), :]] * half, axis=1)
                pltpu.store(field.at[x, r, pl.ds(u, 1), :], current[pl.ds(n, 1), :] + fix, mask=quarter == part)
            return 0

        lax.fori_loop(0, bricks, apply, 0)
        return 0

    lax.fori_loop(0, steps, one_step, 0)
    stores = [
        pltpu.make_async_copy(field.at[pl.ds(place[i] * width + 1, width)], outs[i], load_sem.at[i]) for i in range(bricks)
    ]
    for copy in stores:
        copy.start()
    for copy in stores:
        copy.wait()


def run_steps(place, lists, states, packs, blocks, first, slots, tile):
    with_pack = states is None
    bricks = len(packs)
    _, width, rung, _, depth = packs[0].shape
    planes = bricks * width
    steps = blocks[0].shape[0]
    count = bricks * slots
    body = functools.partial(steps_kernel, (bricks, width, rung, depth), slots, tile, first, with_pack)
    smem = pl.BlockSpec(memory_space=pltpu.SMEM)
    hbm = pl.BlockSpec(memory_space=pl.ANY)
    operands = ([] if with_pack else list(states)) + list(packs) + list(blocks)
    grid_shape = (planes, rung, SUB, depth)
    wide_shape = (planes + 2, rung, SUB, depth)
    packed = blocks[0].shape[2:]
    cells = planes * rung * SUB * depth
    return pl.pallas_call(
        body,
        out_shape=[jax.ShapeDtypeStruct((width, rung, SUB, depth), jnp.float32)] * bricks,
        in_specs=[smem, smem] + [hbm] * len(operands),
        out_specs=[hbm] * bricks,
        scratch_shapes=[
            pltpu.VMEM(wide_shape, jnp.float32),
            pltpu.VMEM(wide_shape, jnp.float32),
            pltpu.VMEM(grid_shape, jnp.float32),
            pltpu.VMEM(grid_shape, jnp.float32),
            pltpu.VMEM(grid_shape, jnp.float32),
            pltpu.VMEM(grid_shape, jnp.float32),
            pltpu.VMEM((count, depth), jnp.float32),
            pltpu.VMEM((count, depth), jnp.float32),
            pltpu.VMEM((count, LANE), jnp.float32),
            pltpu.VMEM((count, LANE), jnp.float32),
            pltpu.VMEM((2, bricks, slots) + packed, jnp.float32),
            pltpu.SemaphoreType.DMA((3 * bricks,)),
            pltpu.SemaphoreType.DMA((2, bricks)),
        ],
        compiler_params=pltpu.CompilerParams(vmem_limit_bytes=60 * 1024 * 1024),
        cost_estimate=pl.CostEstimate(
            flops=cells * steps * SWEEPS * 10, bytes_accessed=cells * 4 * steps * 8, transcendentals=0
        ),
    )(place, lists, *operands)


def routes(windows, bricks):
    home = bricks // 2 - 1
    others = [z for z in range(bricks) if z != home]

    def at(t, z):
        return t * bricks + (z if t % 2 == 0 else bricks - 1 - z)

    rounds = [[(at(t, z), at(t, home)) for t in range(windows)] for z in others]
    return home, others, rounds


def shards(
    opening_guess_profile,
    capacity,
    thermal_forcing,
    rough_decay_factor,
    tile_ids,
    tile_count,
    tile_blocks,
):
    axes = ("tm", "space")
    windows, bricks = lax.axis_size("tm"), lax.axis_size("space")
    window, brick = lax.axis_index("tm"), lax.axis_index("space")
    opening = opening_guess_profile[0]
    rough = rough_decay_factor[0]
    width, rows, depth = opening.shape
    steps, slots = tile_ids.shape
    tile = tile_blocks.shape[-1]
    home, others, rounds = routes(windows, bricks)
    place = jnp.array([home] + others, jnp.int32)
    place = jnp.where(window % 2 == 0, place, bricks - 1 - place)

    rung = rows // SUB
    ids = jnp.concatenate([tile_ids, tile_count], axis=1).astype(jnp.float32)
    ids = lax.all_gather(ids, "space").astype(jnp.int32)
    t, live = ids[..., :slots], jnp.arange(slots) < ids[..., slots:]
    per_row = depth // tile
    line = t // per_row
    plane = line // rows + width * jnp.arange(bricks, dtype=jnp.int32)[:, None, None] + 1
    part = jnp.where(live, t % per_row, -1)
    lists = jnp.stack([plane, line % rung, line % rows // rung, part], axis=-1).reshape(-1)

    pack = jnp.stack([opening, thermal_forcing[0], capacity])
    pack = pack.reshape(3, width, SUB, rung, depth).swapaxes(2, 3)
    group = LANE // tile
    share = tile // group
    blocks = jnp.concatenate([tile_blocks[:, :, g * share : (g + 1) * share] for g in range(group)], axis=-1)
    early = EARLY * steps // 8

    def spread(value):
        return [lax.ppermute(value, axes, pairs) for pairs in rounds]

    def swap(value):
        parts = value.reshape(windows, -1, depth)
        return lax.all_to_all(parts, "tm", 0, 0, tiled=True)

    packs = spread(pack)
    blocks_early = spread(blocks[:early])
    factors = swap(rough)
    place, factors = lax.optimization_barrier((place, factors))
    states = run_steps(
        place, lists, None, [pack] + packs, [blocks[:early]] + blocks_early, 0, slots, tile
    )
    late, _ = lax.optimization_barrier((blocks[early:], packs[-1]))
    blocks_late = spread(late)
    states = run_steps(place, lists, states, [pack] + packs, [late] + blocks_late, early, slots, tile)

    held_here = brick == place[0]
    ending = jnp.where(held_here, states[0], 0.0)
    for pairs, state in zip(rounds, states[1:]):
        ending = ending + lax.ppermute(state, axes, [(b, a) for a, b in pairs])

    ending = ending.swapaxes(1, 2).reshape(width, rows, depth)
    shift = jnp.where(window == 0, ending, ending - rough * opening)
    shifts = swap(shift)
    x = shifts[0]
    arrived = [x]
    for j in range(1, windows):
        arrived.append(x)
        x = factors[j] * x + shifts[j]
    result = swap(jnp.stack(arrived)).reshape(width, rows, depth)
    updated = jnp.where(window == 0, opening, result)
    return (updated[None], ending[None])


def solution(mesh):
    in_specs = (
        P("tm", "space", None, None),
        P("space", None, None),
        P("tm", "space", None, None),
        P("tm", "space", None, None),
        P("tm", "space"),
        P("tm", "space"),
        P("tm", "space", None, None),
    )
    out_specs = (P("tm", "space", None, None), P("tm", "space", None, None))
    return jax.shard_map(shards, mesh=mesh, in_specs=in_specs, out_specs=out_specs, check_vma=False)
```

```python
import functools

import jax
import jax.numpy as jnp
from jax import lax
from jax.experimental import pallas as pl
from jax.experimental.pallas import tpu as pltpu
from jax.sharding import PartitionSpec as P

SWEEPS = 4
COND = 1.0
SUB = 8
LANE = 128
EARLY = 3
SPAN = 8


def span_of(planes):
    return max(n for n in range(1, SPAN + 1) if planes % n == 0)


def steps_kernel(shape, slots, tile, first, steps, own_blocks, *refs):
    bricks, width, rung, depth = shape
    planes, thick = bricks * width, width * rung
    half = depth // LANE
    count = bricks * slots
    share = tile * tile // depth

    def take(n):
        nonlocal refs
        head, refs = refs[:n], refs[n:]
        return head

    (place,) = take(1)
    if own_blocks:
        packs = take(bricks)
        states = [pack.at[pl.ds(0, thick)] for pack in packs]
        blocks = [pack.at[pl.ds(3 * thick, steps * slots * share // SUB)] for pack in packs]
    else:
        states, packs, blocks = take(bricks), take(bricks), take(bricks)
    outs, (mark,) = take(bricks), take(1)
    field, other, source, capacity, inverse, rhs, kept, current, picked, fixes, held, raw, whole_lists, lists, load_sem, held_sem, list_sem = refs
    stack = slots * share // SUB

    def fetch_blocks(step, slot):
        return [
            pltpu.make_async_copy(blocks[i].at[pl.ds(step * stack, stack)], held.at[slot, i], held_sem.at[slot, i])
            for i in range(bricks)
        ]

    def slab(i, lead):
        return pl.ds((place[i] * width + lead) * rung, thick)

    loads = []
    for i in range(bricks):
        loads.append((packs[i].at[pl.ds(2 * thick, thick)], capacity.at[slab(i, 0)]))
    for i in range(bricks):
        loads.append((states[i], field.at[slab(i, 1)]))
        loads.append((packs[i].at[pl.ds(thick, thick)], source.at[slab(i, 0)]))
    loads = [pltpu.make_async_copy(*ends, load_sem.at[n]) for n, ends in enumerate(loads)]
    tail = packs[0].shape[0] - 1
    raw_copies = [pltpu.make_async_copy(packs[i].at[tail], raw.at[i], list_sem.at[i]) for i in range(bricks)]
    for copy in raw_copies:
        copy.start()
    for copy in loads:
        copy.start()
    for copy in fetch_blocks(0, 0):
        copy.start()

    zero = jnp.zeros((rung, SUB, depth), jnp.float32)
    for edge in (0, planes + 1):
        field[pl.ds(edge * rung, rung)] = zero
        other[pl.ds(edge * rung, rung)] = zero
    for copy in raw_copies:
        copy.wait()
    whole_lists[...] = raw[:, : whole_lists.shape[1], :].astype(jnp.int32)
    list_copy = pltpu.make_async_copy(whole_lists, lists, list_sem.at[0])
    list_copy.start()
    for copy in loads[:bricks]:
        copy.wait()

    def invert(x, _):
        plane = pl.ds(x * rung, rung)
        inverse[plane] = 1.0 / (capacity[plane] + 6.0 * COND)
        return 0

    lax.fori_loop(0, planes, invert, 0)
    for copy in loads[bricks:]:
        copy.wait()
    list_copy.wait()

    sub = lax.broadcasted_iota(jnp.int32, (SUB, LANE), 0)
    top, bottom = sub == 0, sub == SUB - 1
    line = lax.broadcasted_iota(jnp.int32, (depth, depth), 0)
    column = lax.broadcasted_iota(jnp.int32, (depth, depth), 1)
    beside = jnp.where(jnp.abs(line - column) == 1, 1.0, 0.0).astype(jnp.bfloat16)
    span = span_of(planes)

    def split(value):
        coarse = value.astype(jnp.bfloat16)
        return coarse, (value - coarse.astype(jnp.float32)).astype(jnp.bfloat16)

    def product(value, matrix):
        coarse, fine = split(value)
        return jnp.dot(coarse, matrix, preferred_element_type=jnp.float32) + jnp.dot(
            fine, matrix, preferred_element_type=jnp.float32
        )

    def sweep(src, dst, opening):
        def chunk(n, _):
            whole = src[pl.ds((n * span + 1) * rung, span * rung)].reshape(span * rung * SUB, depth)
            along = product(whole, beside).reshape(span * rung, SUB, depth)
            for p in range(span):
                x = (n * span + p) * rung
                center = [[src[x + rung + r, :, pl.ds(h * LANE, LANE)] for h in range(half)] for r in range(rung)]
                for r in range(rung):
                    for h in range(half):
                        lanes = pl.ds(h * LANE, LANE)
                        if r:
                            above = center[r - 1][h]
                        else:
                            above = jnp.where(top, 0.0, pltpu.roll(center[rung - 1][h], 1, 0))
                        if r + 1 < rung:
                            below = center[r + 1][h]
                        else:
                            below = jnp.where(bottom, 0.0, pltpu.roll(center[0][h], SUB - 1, 0))
                        total = src[x + r, :, lanes] + src[x + 2 * rung + r, :, lanes]
                        total = total + (above + below) + along[p * rung + r, :, h * LANE : (h + 1) * LANE]
                        if opening:
                            base = capacity[x + r, :, lanes] * center[r][h] + source[x + r, :, lanes]
                            rhs[x + r, :, lanes] = base
                        else:
                            base = rhs[x + r, :, lanes]
                        dst[x + rung + r, :, lanes] = (base + COND * total) * inverse[x + r, :, lanes]
            return 0

        lax.fori_loop(0, planes // span, chunk, 0)

    quarter = lax.broadcasted_iota(jnp.int32, (1, depth), 1) // tile
    group = depth // tile
    gathers = jnp.where(line // tile == (column % tile) // share, 1.0, 0.0).astype(jnp.bfloat16)
    own_line = lax.broadcasted_iota(jnp.int32, (share, depth), 0)
    own_lane = lax.broadcasted_iota(jnp.int32, (share, depth), 1)
    diagonal = own_line == own_lane % share
    tiles = [(i, s) for i in range(bricks) for s in range(slots)]

    def cell_of(step, i, s):
        at = ((first + step) * slots + s) * 4
        spot = [lists[i, (at + k) // depth, (at + k) % depth] for k in range(3)]
        return spot[0] + (place[i] * width + 1) * rung, spot[1], spot[2]

    def one_step(step, _):
        slot = step % 2

        @pl.when(step + 1 < steps)
        def _():
            for copy in fetch_blocks(step + 1, 1 - slot):
                copy.start()

        for n, (i, s) in enumerate(tiles):
            x, u, _unused = cell_of(step, i, s)
            kept[n : n + 1, :] = field[x, pl.ds(u, 1), :]
        sweep(field, other, True)
        for _pair in range((SWEEPS - 2) // 2):
            sweep(other, field, False)
            sweep(field, other, False)
        sweep(other, field, False)

        for n, (i, s) in enumerate(tiles):
            x, u, part = cell_of(step, i, s)
            value = field[x, pl.ds(u, 1), :]
            current[n : n + 1, :] = value
            delta = jnp.where(quarter == part, value - kept[n : n + 1, :], 0.0)
            whole = delta
            for g in range(1, group):
                whole = whole + pltpu.roll(delta, g * tile, 1)
            picked[n : n + 1, :] = whole
        for copy in fetch_blocks(step, slot):
            copy.wait()

        def multiply(b, _):
            terms = [
                held[slot, b, pl.ds(s * (share // SUB), share // SUB)].reshape(share, depth)
                * picked[pl.ds(b * slots + s, 1), :]
                for s in range(slots)
            ]
            sums = product(jnp.concatenate(terms, axis=0), gathers)
            for s in range(slots):
                fix = jnp.where(diagonal, sums[s * share : (s + 1) * share], 0.0)
                fixes[pl.ds(b * slots + s, 1), :] = jnp.sum(fix, axis=0, keepdims=True)
            return 0

        lax.fori_loop(0, bricks, multiply, 0)

        for n, (i, s) in enumerate(tiles):
            x, u, part = cell_of(step, i, s)
            value = current[n : n + 1, :] + fixes[n : n + 1, :]
            pltpu.store(field.at[x, pl.ds(u, 1), :], value, mask=quarter == part)
        return 0

    lax.fori_loop(0, steps, one_step, 0)
    stores = [
        pltpu.make_async_copy(field.at[slab(i, 1)], outs[i], load_sem.at[i]) for i in range(bricks)
    ]
    for copy in stores:
        copy.start()
    mark[...] = jnp.zeros_like(mark)
    for copy in stores:
        copy.wait()


def run_steps(place, states, packs, blocks, shape, list_rows, first, steps, slots, tile):
    bricks, width, rung, depth = shape
    planes = bricks * width
    count = bricks * slots
    body = functools.partial(steps_kernel, shape, slots, tile, first, steps, blocks is None)
    smem = pl.BlockSpec(memory_space=pltpu.SMEM)
    hbm = pl.BlockSpec(memory_space=pl.ANY)
    operands = list(packs) if blocks is None else list(states) + list(packs) + list(blocks)
    grid_shape = (planes * rung, SUB, depth)
    wide_shape = ((planes + 2) * rung, SUB, depth)
    cells = planes * rung * SUB * depth
    return pl.pallas_call(
        body,
        out_shape=[jax.ShapeDtypeStruct((width * rung, SUB, depth), jnp.float32)] * bricks
        + [jax.ShapeDtypeStruct((SUB, LANE), jnp.float32)],
        in_specs=[smem] + [hbm] * len(operands),
        out_specs=[hbm] * bricks + [pl.BlockSpec(memory_space=pltpu.VMEM)],
        scratch_shapes=[
            pltpu.VMEM(wide_shape, jnp.float32),
            pltpu.VMEM(wide_shape, jnp.float32),
            pltpu.VMEM(grid_shape, jnp.float32),
            pltpu.VMEM(grid_shape, jnp.float32),
            pltpu.VMEM(grid_shape, jnp.float32),
            pltpu.VMEM(grid_shape, jnp.float32),
            pltpu.VMEM((count, depth), jnp.float32),
            pltpu.VMEM((count, depth), jnp.float32),
            pltpu.VMEM((count, depth), jnp.float32),
            pltpu.VMEM((count, depth), jnp.float32),
            pltpu.VMEM((2, bricks, slots * tile * tile // depth // SUB, SUB, depth), jnp.float32),
            pltpu.VMEM((bricks, SUB, depth), jnp.float32),
            pltpu.VMEM((bricks, list_rows, depth), jnp.int32),
            pltpu.SMEM((bricks, list_rows, depth), jnp.int32),
            pltpu.SemaphoreType.DMA((3 * bricks,)),
            pltpu.SemaphoreType.DMA((2, bricks)),
            pltpu.SemaphoreType.DMA((bricks,)),
        ],
        compiler_params=pltpu.CompilerParams(vmem_limit_bytes=60 * 1024 * 1024),
        cost_estimate=pl.CostEstimate(
            flops=cells * steps * SWEEPS * 10, bytes_accessed=cells * 4 * steps * 8, transcendentals=0
        ),
    )(place, *operands)


def recurrence(factors, shifts):
    def body(factor, shift, out):
        x = shift[0]
        out[0] = x
        for j in range(1, shifts.shape[0]):
            out[j] = x
            x = factor[j] * x + shift[j]

    return pl.pallas_call(body, out_shape=jax.ShapeDtypeStruct(shifts.shape, jnp.float32))(factors, shifts)


def routes(windows, bricks):
    home = bricks // 2 - 1
    others = [z for z in range(bricks) if z != home]

    def at(t, z):
        return t * bricks + (z if t % 2 == 0 else bricks - 1 - z)

    rounds = [[(at(t, z), at(t, home)) for t in range(windows)] for z in others]
    return home, others, rounds


def shards(
    opening_guess_profile,
    capacity,
    thermal_forcing,
    rough_decay_factor,
    tile_ids,
    tile_count,
    tile_blocks,
):
    axes = ("tm", "space")
    windows, bricks = lax.axis_size("tm"), lax.axis_size("space")
    window, brick = lax.axis_index("tm"), lax.axis_index("space")
    opening = opening_guess_profile[0]
    rough = rough_decay_factor[0]
    width, rows, depth = opening.shape
    steps, slots = tile_ids.shape
    tile = tile_blocks.shape[-1]
    home, others, rounds = routes(windows, bricks)
    place = jnp.array([home] + others, jnp.int32)
    place = jnp.where(window % 2 == 0, place, bricks - 1 - place)

    rung = rows // SUB
    live = jnp.arange(slots) < tile_count
    per_row = depth // tile
    line = tile_ids // per_row
    part = jnp.where(live, tile_ids % per_row, -1)
    cells = jnp.stack([line // rows * rung + line % rung, line % rows // rung, part, part], axis=-1)
    cells = cells.astype(jnp.float32).reshape(-1, depth)
    list_rows = cells.shape[0]
    cells = jnp.pad(cells, ((0, SUB - cells.shape[0]), (0, 0)))[None]

    def blocked(value):
        return value.reshape(-1, SUB, rung, depth).swapaxes(1, 2).reshape(-1, SUB, depth)

    group = depth // tile
    share = tile // group
    blocks = jnp.concatenate([tile_blocks[:, :, g * share : (g + 1) * share] for g in range(group)], axis=-1)
    blocks = blocks.reshape(-1, SUB, depth)
    early = EARLY * steps // 8
    cut = early * (blocks.shape[0] // steps)
    fields = [blocked(value) for value in (opening, thermal_forcing[0], capacity)]
    pack = jnp.concatenate(fields + [blocks[:cut], cells])
    shape = (bricks, width, rung, depth)

    def spread(value):
        return [lax.ppermute(value, axes, pairs) for pairs in rounds]

    def swap(value):
        parts = value.reshape(windows, -1, depth)
        return lax.all_to_all(parts, "tm", 0, 0, tiled=True)

    packs = [pack] + spread(pack)
    blocks_late = [blocks[cut:]] + spread(blocks[cut:])
    *states, mark = run_steps(place, None, packs, None, shape, list_rows, 0, early, slots, tile)
    rough_late, _ = lax.optimization_barrier((rough, mark))
    factors = lax.all_gather(rough_late, "tm").reshape(windows, windows, -1, depth)
    factors = lax.dynamic_index_in_dim(factors, window, 1, keepdims=False)
    *states, mark = run_steps(place, states, packs, blocks_late, shape, list_rows, early, steps - early, slots, tile)

    held_here = brick == place[0]
    ending = jnp.where(held_here, states[0], 0.0)
    for pairs, state in zip(rounds, states[1:]):
        ending = ending + lax.ppermute(state, axes, [(b, a) for a, b in pairs])

    ending = ending.reshape(width, rung, SUB, depth).swapaxes(1, 2).reshape(width, rows, depth)
    shift = jnp.where(window == 0, ending, ending - rough * opening)
    shifts = swap(shift)
    result = swap(recurrence(factors, shifts)).reshape(width, rows, depth)
    updated = jnp.where(window == 0, opening, result)
    return (updated[None], ending[None])


def solution(mesh):
    in_specs = (
        P("tm", "space", None, None),
        P("space", None, None),
        P("tm", "space", None, None),
        P("tm", "space", None, None),
        P("tm", "space"),
        P("tm", "space"),
        P("tm", "space", None, None),
    )
    out_specs = (P("tm", "space", None, None), P("tm", "space", None, None))
    return jax.shard_map(shards, mesh=mesh, in_specs=in_specs, out_specs=out_specs, check_vma=False)
```

```python
import functools

import jax
import jax.numpy as jnp
from jax import lax
from jax.experimental import pallas as pl
from jax.experimental.pallas import tpu as pltpu
from jax.sharding import PartitionSpec as P

SWEEPS = 4
COND = 1.0
SUB = 8
LANE = 128
EARLY = 2
SPAN = 8


def span_of(planes):
    return max(n for n in range(1, SPAN + 1) if planes % n == 0)


def steps_kernel(shape, slots, tile, first, steps, own_blocks, *refs):
    bricks, width, rung, depth = shape
    planes, thick = bricks * width, width * rung
    half = depth // LANE
    count = bricks * slots
    share = tile * tile // depth

    def take(n):
        nonlocal refs
        head, refs = refs[:n], refs[n:]
        return head

    (place,) = take(1)
    if own_blocks:
        packs = take(bricks)
        states = [pack.at[pl.ds(0, thick)] for pack in packs]
        blocks = [pack.at[pl.ds(3 * thick, steps * slots * share // SUB)] for pack in packs]
    else:
        states, packs, blocks = take(bricks), take(bricks), take(bricks)
    outs = take(bricks)
    field, other, source, capacity, inverse, rhs, kept, current, picked, fixes, held, raw, whole_lists, lists, load_sem, held_sem, list_sem = refs
    stack = slots * share // SUB

    def fetch_blocks(step, slot):
        return [
            pltpu.make_async_copy(blocks[i].at[pl.ds(step * stack, stack)], held.at[slot, i], held_sem.at[slot, i])
            for i in range(bricks)
        ]

    def slab(i, lead):
        return pl.ds((place[i] * width + lead) * rung, thick)

    loads = []
    for i in range(bricks):
        loads.append((packs[i].at[pl.ds(2 * thick, thick)], capacity.at[slab(i, 0)]))
    for i in range(bricks):
        loads.append((states[i], field.at[slab(i, 1)]))
        loads.append((packs[i].at[pl.ds(thick, thick)], source.at[slab(i, 0)]))
    loads = [pltpu.make_async_copy(*ends, load_sem.at[n]) for n, ends in enumerate(loads)]
    tail = packs[0].shape[0] - 1
    raw_copies = [pltpu.make_async_copy(packs[i].at[tail], raw.at[i], list_sem.at[i]) for i in range(bricks)]
    for copy in raw_copies:
        copy.start()
    for copy in loads:
        copy.start()
    for copy in fetch_blocks(0, 0):
        copy.start()

    zero = jnp.zeros((rung, SUB, depth), jnp.float32)
    for edge in (0, planes + 1):
        field[pl.ds(edge * rung, rung)] = zero
        other[pl.ds(edge * rung, rung)] = zero
    for copy in raw_copies:
        copy.wait()
    whole_lists[...] = raw[:, : whole_lists.shape[1], :].astype(jnp.int32)
    list_copy = pltpu.make_async_copy(whole_lists, lists, list_sem.at[0])
    list_copy.start()
    for copy in loads[:bricks]:
        copy.wait()

    def invert(x, _):
        plane = pl.ds(x * rung, rung)
        inverse[plane] = 1.0 / (capacity[plane] + 6.0 * COND)
        return 0

    lax.fori_loop(0, planes, invert, 0)
    for copy in loads[bricks:]:
        copy.wait()
    list_copy.wait()

    sub = lax.broadcasted_iota(jnp.int32, (SUB, LANE), 0)
    top, bottom = sub == 0, sub == SUB - 1
    line = lax.broadcasted_iota(jnp.int32, (depth, depth), 0)
    column = lax.broadcasted_iota(jnp.int32, (depth, depth), 1)
    beside = jnp.where(jnp.abs(line - column) == 1, 1.0, 0.0).astype(jnp.bfloat16)
    span = span_of(planes)

    def split(value):
        coarse = value.astype(jnp.bfloat16)
        return coarse, (value - coarse.astype(jnp.float32)).astype(jnp.bfloat16)

    def product(value, matrix):
        coarse, fine = split(value)
        return jnp.dot(coarse, matrix, preferred_element_type=jnp.float32) + jnp.dot(
            fine, matrix, preferred_element_type=jnp.float32
        )

    def sweep(src, dst, opening):
        def chunk(n, _):
            whole = src[pl.ds((n * span + 1) * rung, span * rung)].reshape(span * rung * SUB, depth)
            along = product(whole, beside).reshape(span * rung, SUB, depth)
            for p in range(span):
                x = (n * span + p) * rung
                center = [[src[x + rung + r, :, pl.ds(h * LANE, LANE)] for h in range(half)] for r in range(rung)]
                for r in range(rung):
                    for h in range(half):
                        lanes = pl.ds(h * LANE, LANE)
                        if r:
                            above = center[r - 1][h]
                        else:
                            above = jnp.where(top, 0.0, pltpu.roll(center[rung - 1][h], 1, 0))
                        if r + 1 < rung:
                            below = center[r + 1][h]
                        else:
                            below = jnp.where(bottom, 0.0, pltpu.roll(center[0][h], SUB - 1, 0))
                        total = src[x + r, :, lanes] + src[x + 2 * rung + r, :, lanes]
                        total = total + (above + below) + along[p * rung + r, :, h * LANE : (h + 1) * LANE]
                        if opening:
                            base = capacity[x + r, :, lanes] * center[r][h] + source[x + r, :, lanes]
                            rhs[x + r, :, lanes] = base
                        else:
                            base = rhs[x + r, :, lanes]
                        dst[x + rung + r, :, lanes] = (base + COND * total) * inverse[x + r, :, lanes]
            return 0

        lax.fori_loop(0, planes // span, chunk, 0)

    quarter = lax.broadcasted_iota(jnp.int32, (1, depth), 1) // tile
    group = depth // tile
    gathers = jnp.where(line // tile == (column % tile) // share, 1.0, 0.0).astype(jnp.bfloat16)
    own_line = lax.broadcasted_iota(jnp.int32, (share, depth), 0)
    own_lane = lax.broadcasted_iota(jnp.int32, (share, depth), 1)
    diagonal = own_line == own_lane % share
    tiles = [(i, s) for i in range(bricks) for s in range(slots)]

    def cell_of(step, i, s):
        at = ((first + step) * slots + s) * 4
        spot = [lists[i, (at + k) // depth, (at + k) % depth] for k in range(3)]
        return spot[0] + (place[i] * width + 1) * rung, spot[1], spot[2]

    def one_step(step, _):
        slot = step % 2

        @pl.when(step + 1 < steps)
        def _():
            for copy in fetch_blocks(step + 1, 1 - slot):
                copy.start()

        for n, (i, s) in enumerate(tiles):
            x, u, _unused = cell_of(step, i, s)
            kept[n : n + 1, :] = field[x, pl.ds(u, 1), :]
        sweep(field, other, True)
        for _pair in range((SWEEPS - 2) // 2):
            sweep(other, field, False)
            sweep(field, other, False)
        sweep(other, field, False)

        for n, (i, s) in enumerate(tiles):
            x, u, part = cell_of(step, i, s)
            value = field[x, pl.ds(u, 1), :]
            current[n : n + 1, :] = value
            delta = jnp.where(quarter == part, value - kept[n : n + 1, :], 0.0)
            whole = delta
            for g in range(1, group):
                whole = whole + pltpu.roll(delta, g * tile, 1)
            picked[n : n + 1, :] = whole
        for copy in fetch_blocks(step, slot):
            copy.wait()

        def multiply(b, _):
            terms = [
                held[slot, b, pl.ds(s * (share // SUB), share // SUB)].reshape(share, depth)
                * picked[pl.ds(b * slots + s, 1), :]
                for s in range(slots)
            ]
            sums = product(jnp.concatenate(terms, axis=0), gathers)
            for s in range(slots):
                fix = jnp.where(diagonal, sums[s * share : (s + 1) * share], 0.0)
                fixes[pl.ds(b * slots + s, 1), :] = jnp.sum(fix, axis=0, keepdims=True)
            return 0

        lax.fori_loop(0, bricks, multiply, 0)

        for n, (i, s) in enumerate(tiles):
            x, u, part = cell_of(step, i, s)
            value = current[n : n + 1, :] + fixes[n : n + 1, :]
            pltpu.store(field.at[x, pl.ds(u, 1), :], value, mask=quarter == part)
        return 0

    lax.fori_loop(0, steps, one_step, 0)
    stores = [
        pltpu.make_async_copy(field.at[slab(i, 1)], outs[i], load_sem.at[i]) for i in range(bricks)
    ]
    for copy in stores:
        copy.start()
    for copy in stores:
        copy.wait()


def run_steps(place, states, packs, blocks, shape, list_rows, first, steps, slots, tile):
    bricks, width, rung, depth = shape
    planes = bricks * width
    count = bricks * slots
    body = functools.partial(steps_kernel, shape, slots, tile, first, steps, blocks is None)
    smem = pl.BlockSpec(memory_space=pltpu.SMEM)
    hbm = pl.BlockSpec(memory_space=pl.ANY)
    operands = list(packs) if blocks is None else list(states) + list(packs) + list(blocks)
    grid_shape = (planes * rung, SUB, depth)
    wide_shape = ((planes + 2) * rung, SUB, depth)
    cells = planes * rung * SUB * depth
    return pl.pallas_call(
        body,
        out_shape=[jax.ShapeDtypeStruct((width * rung, SUB, depth), jnp.float32)] * bricks,
        in_specs=[smem] + [hbm] * len(operands),
        out_specs=[hbm] * bricks,
        scratch_shapes=[
            pltpu.VMEM(wide_shape, jnp.float32),
            pltpu.VMEM(wide_shape, jnp.float32),
            pltpu.VMEM(grid_shape, jnp.float32),
            pltpu.VMEM(grid_shape, jnp.float32),
            pltpu.VMEM(grid_shape, jnp.float32),
            pltpu.VMEM(grid_shape, jnp.float32),
            pltpu.VMEM((count, depth), jnp.float32),
            pltpu.VMEM((count, depth), jnp.float32),
            pltpu.VMEM((count, depth), jnp.float32),
            pltpu.VMEM((count, depth), jnp.float32),
            pltpu.VMEM((2, bricks, slots * tile * tile // depth // SUB, SUB, depth), jnp.float32),
            pltpu.VMEM((bricks, SUB, depth), jnp.float32),
            pltpu.VMEM((bricks, list_rows, depth), jnp.int32),
            pltpu.SMEM((bricks, list_rows, depth), jnp.int32),
            pltpu.SemaphoreType.DMA((3 * bricks,)),
            pltpu.SemaphoreType.DMA((2, bricks)),
            pltpu.SemaphoreType.DMA((bricks,)),
        ],
        compiler_params=pltpu.CompilerParams(vmem_limit_bytes=60 * 1024 * 1024),
        cost_estimate=pl.CostEstimate(
            flops=cells * steps * SWEEPS * 10, bytes_accessed=cells * 4 * steps * 8, transcendentals=0
        ),
    )(place, *operands)


def recurrence(parts):
    windows, lines, depth = parts.shape
    share = lines // 2

    def body(part, out):
        x = part[0, :share]
        out[0] = x
        for j in range(1, windows):
            out[j] = x
            x = part[j, share:] * x + part[j, :share]

    return pl.pallas_call(body, out_shape=jax.ShapeDtypeStruct((windows, share, depth), jnp.float32))(parts)


def routes(windows, bricks):
    home = bricks // 2 - 1
    others = [z for z in range(home + 1, bricks)] + [z for z in range(home)]

    def at(t, z):
        return t * bricks + (z if t % 2 == 0 else bricks - 1 - z)

    rounds = [[(at(t, z), at(t, home)) for t in range(windows)] for z in others]
    return home, others, rounds


def shards(
    opening_guess_profile,
    capacity,
    thermal_forcing,
    rough_decay_factor,
    tile_ids,
    tile_count,
    tile_blocks,
):
    axes = ("tm", "space")
    windows, bricks = lax.axis_size("tm"), lax.axis_size("space")
    window, brick = lax.axis_index("tm"), lax.axis_index("space")
    opening = opening_guess_profile[0]
    rough = rough_decay_factor[0]
    width, rows, depth = opening.shape
    steps, slots = tile_ids.shape
    tile = tile_blocks.shape[-1]
    home, others, rounds = routes(windows, bricks)
    place = jnp.array([home] + others, jnp.int32)
    place = jnp.where(window % 2 == 0, place, bricks - 1 - place)

    rung = rows // SUB
    live = jnp.arange(slots) < tile_count
    per_row = depth // tile
    line = tile_ids // per_row
    part = jnp.where(live, tile_ids % per_row, -1)
    cells = jnp.stack([line // rows * rung + line % rung, line % rows // rung, part, part], axis=-1)
    cells = cells.astype(jnp.float32).reshape(-1, depth)
    list_rows = cells.shape[0]
    cells = jnp.pad(cells, ((0, SUB - cells.shape[0]), (0, 0)))[None]

    def blocked(value):
        return value.reshape(-1, SUB, rung, depth).swapaxes(1, 2).reshape(-1, SUB, depth)

    group = depth // tile
    share = tile // group
    blocks = jnp.concatenate([tile_blocks[:, :, g * share : (g + 1) * share] for g in range(group)], axis=-1)
    blocks = blocks.reshape(-1, SUB, depth)
    early = EARLY * steps // 8
    cut = early * (blocks.shape[0] // steps)
    fields = [blocked(value) for value in (opening, thermal_forcing[0], capacity)]
    pack = jnp.concatenate(fields + [blocks[:cut], cells])
    shape = (bricks, width, rung, depth)

    def spread(value):
        return [lax.ppermute(value, axes, pairs) for pairs in rounds]

    def swap(value):
        return lax.all_to_all(value, "tm", 0, 0, tiled=True)

    packs = [pack] + spread(pack)
    blocks_late = [blocks[cut:]] + spread(blocks[cut:])
    states = run_steps(place, None, packs, None, shape, list_rows, 0, early, slots, tile)
    states = run_steps(place, states, packs, blocks_late, shape, list_rows, early, steps - early, slots, tile)

    held_here = brick == place[0]
    ending = jnp.where(held_here, states[0], 0.0)
    for pairs, state in reversed(list(zip(rounds, states[1:]))):
        ending = ending + lax.ppermute(state, axes, [(b, a) for a, b in pairs])

    ending = ending.reshape(width, rung, SUB, depth).swapaxes(1, 2).reshape(width, rows, depth)
    shift = jnp.where(window == 0, ending, ending - rough * opening)
    parts = jnp.concatenate([shift.reshape(windows, -1, depth), rough.reshape(windows, -1, depth)], axis=1)
    result = swap(recurrence(swap(parts))).reshape(width, rows, depth)
    updated = jnp.where(window == 0, opening, result)
    return (updated[None], ending[None])


def solution(mesh):
    in_specs = (
        P("tm", "space", None, None),
        P("space", None, None),
        P("tm", "space", None, None),
        P("tm", "space", None, None),
        P("tm", "space"),
        P("tm", "space"),
        P("tm", "space", None, None),
    )
    out_specs = (P("tm", "space", None, None), P("tm", "space", None, None))
    return jax.shard_map(shards, mesh=mesh, in_specs=in_specs, out_specs=out_specs, check_vma=False)
```

```python
import functools

import jax
import jax.numpy as jnp
from jax import lax
from jax.experimental import pallas as pl
from jax.experimental.pallas import tpu as pltpu
from jax.sharding import PartitionSpec as P

SWEEPS = 4
COND = 1.0
SUB = 8
LANE = 128
EARLY = 2
SPAN = 4
CHUNKS = 4


def span_of(planes, most):
    return max(n for n in range(1, most + 1) if planes % n == 0)


def steps_kernel(shape, slots, tile, first, steps, own_blocks, *refs):
    bricks, width, rung, depth = shape
    planes, thick = bricks * width, width * rung
    half = depth // LANE
    count = bricks * slots
    share = tile * tile // depth

    def take(n):
        nonlocal refs
        head, refs = refs[:n], refs[n:]
        return head

    (place,) = take(1)
    if own_blocks:
        packs = take(bricks)
        states = [pack.at[pl.ds(0, thick)] for pack in packs]
        blocks = [pack.at[pl.ds(3 * thick, steps * slots * share // SUB)] for pack in packs]
    else:
        states, packs, blocks = take(bricks), take(bricks), take(bricks)
    outs = take(bricks)
    field, other, source, capacity, inverse, rhs, kept, current, picked, fixes, held, raw, whole_lists, lists, load_sem, held_sem, list_sem = refs
    stack = slots * share // SUB

    def fetch_blocks(step, slot):
        return [
            pltpu.make_async_copy(blocks[i].at[pl.ds(step * stack, stack)], held.at[slot, i], held_sem.at[slot, i])
            for i in range(bricks)
        ]

    def slab(i, lead):
        return pl.ds((place[i] * width + lead) * rung, thick)

    loads = []
    for i in range(bricks):
        loads.append((packs[i].at[pl.ds(2 * thick, thick)], capacity.at[slab(i, 0)]))
    for i in range(bricks):
        loads.append((states[i], field.at[slab(i, 1)]))
        loads.append((packs[i].at[pl.ds(thick, thick)], source.at[slab(i, 0)]))
    loads = [pltpu.make_async_copy(*ends, load_sem.at[n]) for n, ends in enumerate(loads)]
    tail = packs[0].shape[0] - 1
    raw_copies = [pltpu.make_async_copy(packs[i].at[tail], raw.at[i], list_sem.at[i]) for i in range(bricks)]
    for copy in raw_copies:
        copy.start()
    for copy in loads:
        copy.start()
    for copy in fetch_blocks(0, 0):
        copy.start()

    zero = jnp.zeros((rung, SUB, depth), jnp.float32)
    for edge in (0, planes + 1):
        field[pl.ds(edge * rung, rung)] = zero
        other[pl.ds(edge * rung, rung)] = zero
    for copy in raw_copies:
        copy.wait()
    whole_lists[...] = raw[:, : whole_lists.shape[1], :].astype(jnp.int32)
    list_copy = pltpu.make_async_copy(whole_lists, lists, list_sem.at[0])
    list_copy.start()
    for copy in loads[:bricks]:
        copy.wait()

    def invert(x, _):
        plane = pl.ds(x * rung, rung)
        inverse[plane] = 1.0 / (capacity[plane] + 6.0 * COND)
        return 0

    lax.fori_loop(0, planes, invert, 0)
    for copy in loads[bricks:]:
        copy.wait()
    list_copy.wait()

    sub = lax.broadcasted_iota(jnp.int32, (SUB, LANE), 0)
    top, bottom = sub == 0, sub == SUB - 1
    line = lax.broadcasted_iota(jnp.int32, (depth, depth), 0)
    column = lax.broadcasted_iota(jnp.int32, (depth, depth), 1)
    beside = jnp.where(jnp.abs(line - column) == 1, 1.0, 0.0).astype(jnp.bfloat16)
    span = span_of(planes, SPAN)
    chunks = span_of(planes // span, CHUNKS)

    def split(value):
        coarse = value.astype(jnp.bfloat16)
        return coarse, (value - coarse.astype(jnp.float32)).astype(jnp.bfloat16)

    def product(value, matrix):
        coarse, fine = split(value)
        return jnp.dot(coarse, matrix, preferred_element_type=jnp.float32) + jnp.dot(
            fine, matrix, preferred_element_type=jnp.float32
        )

    def sweep(src, dst, opening):
        def sides_of(n):
            whole = src[pl.ds((n * span + 1) * rung, span * rung)].reshape(span * rung * SUB, depth)
            return product(whole, beside).reshape(span * rung, SUB, depth)

        def update(n, along):
            base = n * span * rung
            for h in range(half):
                lanes = pl.ds(h * LANE, LANE)

                def line_of(r, lead, tail):
                    return [src[base + q * rung + r, :, lanes] for q in range(lead, span + 2 - tail)]

                above = [jnp.where(top, 0.0, pltpu.roll(v, 1, 0)) for v in line_of(rung - 1, 1, 1)]
                line = line_of(0, 0, 0)
                for r in range(rung):
                    if r + 1 < rung:
                        after = line_of(r + 1, 0, 0)
                        below = after[1:-1]
                    else:
                        after = None
                        below = [jnp.where(bottom, 0.0, pltpu.roll(v, SUB - 1, 0)) for v in line_of(0, 1, 1)]
                    for p in range(span):
                        at = base + p * rung + r
                        total = (line[p] + line[p + 2]) + (above[p] + below[p])
                        total = total + along[p * rung + r, :, h * LANE : (h + 1) * LANE]
                        if opening:
                            start = capacity[at, :, lanes] * line[p + 1] + source[at, :, lanes]
                            rhs[at, :, lanes] = start
                        else:
                            start = rhs[at, :, lanes]
                        dst[at + rung, :, lanes] = (start + COND * total) * inverse[at, :, lanes]
                    above, line = line[1:-1], after

        def batch(m, _):
            along = sides_of(m * chunks)
            for n in range(chunks):
                coming = sides_of(m * chunks + n + 1) if n + 1 < chunks else None
                update(m * chunks + n, along)
                along = coming
            return 0

        lax.fori_loop(0, planes // (span * chunks), batch, 0)

    quarter = lax.broadcasted_iota(jnp.int32, (1, depth), 1) // tile
    group = depth // tile
    gathers = jnp.where(line // tile == (column % tile) // share, 1.0, 0.0).astype(jnp.bfloat16)
    repeats = jnp.where(line % tile == column % tile, 1.0, 0.0).astype(jnp.bfloat16)
    own_line = lax.broadcasted_iota(jnp.int32, (share, depth), 0)
    own_lane = lax.broadcasted_iota(jnp.int32, (share, depth), 1)
    diagonal = own_line == own_lane % share
    tiles = [(i, s) for i in range(bricks) for s in range(slots)]

    def cell_of(step, i, s):
        at = ((first + step) * slots + s) * 4
        spot = [lists[i, (at + k) // depth, (at + k) % depth] for k in range(3)]
        return spot[0] + (place[i] * width + 1) * rung, spot[1], spot[2]

    def one_step(step, _):
        slot = step % 2

        @pl.when(step + 1 < steps)
        def _():
            for copy in fetch_blocks(step + 1, 1 - slot):
                copy.start()

        for n, (i, s) in enumerate(tiles):
            x, u, _unused = cell_of(step, i, s)
            kept[n : n + 1, :] = field[x, pl.ds(u, 1), :]
        sweep(field, other, True)
        for _pair in range((SWEEPS - 2) // 2):
            sweep(other, field, False)
            sweep(field, other, False)
        sweep(other, field, False)

        for n, (i, s) in enumerate(tiles):
            x, u, part = cell_of(step, i, s)
            value = field[x, pl.ds(u, 1), :]
            current[n : n + 1, :] = value
            delta = jnp.where(quarter == part, value - kept[n : n + 1, :], 0.0)
            picked[n : n + 1, :] = delta
        for copy in fetch_blocks(step, slot):
            copy.wait()

        picked[...] = product(picked[...], repeats)
        thin = share // SUB
        terms = []
        for n, (i, s) in enumerate(tiles):
            block = held[slot, i, pl.ds(s * thin, thin)].reshape(share, depth)
            terms.append(block * picked[n : n + 1, :])
        sums = product(jnp.concatenate(terms, axis=0), gathers)
        for n in range(count):
            fix = jnp.where(diagonal, sums[n * share : (n + 1) * share], 0.0)
            fixes[n : n + 1, :] = jnp.sum(fix, axis=0, keepdims=True)

        for n, (i, s) in enumerate(tiles):
            x, u, part = cell_of(step, i, s)
            value = current[n : n + 1, :] + fixes[n : n + 1, :]
            pltpu.store(field.at[x, pl.ds(u, 1), :], value, mask=quarter == part)
        return 0

    lax.fori_loop(0, steps, one_step, 0)
    stores = [
        pltpu.make_async_copy(field.at[slab(i, 1)], outs[i], load_sem.at[i]) for i in range(bricks)
    ]
    for copy in stores:
        copy.start()
    for copy in stores:
        copy.wait()


def run_steps(place, states, packs, blocks, shape, list_rows, first, steps, slots, tile):
    bricks, width, rung, depth = shape
    planes = bricks * width
    count = bricks * slots
    body = functools.partial(steps_kernel, shape, slots, tile, first, steps, blocks is None)
    smem = pl.BlockSpec(memory_space=pltpu.SMEM)
    hbm = pl.BlockSpec(memory_space=pl.ANY)
    operands = list(packs) if blocks is None else list(states) + list(packs) + list(blocks)
    grid_shape = (planes * rung, SUB, depth)
    wide_shape = ((planes + 2) * rung, SUB, depth)
    cells = planes * rung * SUB * depth
    return pl.pallas_call(
        body,
        out_shape=[jax.ShapeDtypeStruct((width * rung, SUB, depth), jnp.float32)] * bricks,
        in_specs=[smem] + [hbm] * len(operands),
        out_specs=[hbm] * bricks,
        scratch_shapes=[
            pltpu.VMEM(wide_shape, jnp.float32),
            pltpu.VMEM(wide_shape, jnp.float32),
            pltpu.VMEM(grid_shape, jnp.float32),
            pltpu.VMEM(grid_shape, jnp.float32),
            pltpu.VMEM(grid_shape, jnp.float32),
            pltpu.VMEM(grid_shape, jnp.float32),
            pltpu.VMEM((count, depth), jnp.float32),
            pltpu.VMEM((count, depth), jnp.float32),
            pltpu.VMEM((count, depth), jnp.float32),
            pltpu.VMEM((count, depth), jnp.float32),
            pltpu.VMEM((2, bricks, slots * tile * tile // depth // SUB, SUB, depth), jnp.float32),
            pltpu.VMEM((bricks, SUB, depth), jnp.float32),
            pltpu.VMEM((bricks, list_rows, depth), jnp.int32),
            pltpu.SMEM((bricks, list_rows, depth), jnp.int32),
            pltpu.SemaphoreType.DMA((3 * bricks,)),
            pltpu.SemaphoreType.DMA((2, bricks)),
            pltpu.SemaphoreType.DMA((bricks,)),
        ],
        compiler_params=pltpu.CompilerParams(vmem_limit_bytes=60 * 1024 * 1024),
        cost_estimate=pl.CostEstimate(
            flops=cells * steps * SWEEPS * 10, bytes_accessed=cells * 4 * steps * 8, transcendentals=0
        ),
    )(place, *operands)


def recurrence(parts):
    windows, lines, depth = parts.shape
    share = lines // 2

    def body(part, out):
        x = part[0, :share]
        out[0] = x
        for j in range(1, windows):
            out[j] = x
            x = part[j, share:] * x + part[j, :share]

    return pl.pallas_call(body, out_shape=jax.ShapeDtypeStruct((windows, share, depth), jnp.float32))(parts)


def routes(windows, bricks):
    home = bricks // 2 - 1
    others = [z for z in range(home + 1, bricks)] + [z for z in range(home)]

    def at(t, z):
        return t * bricks + (z if t % 2 == 0 else bricks - 1 - z)

    rounds = [[(at(t, z), at(t, home)) for t in range(windows)] for z in others]
    return home, others, rounds


def shards(
    opening_guess_profile,
    capacity,
    thermal_forcing,
    rough_decay_factor,
    tile_ids,
    tile_count,
    tile_blocks,
):
    axes = ("tm", "space")
    windows, bricks = lax.axis_size("tm"), lax.axis_size("space")
    window, brick = lax.axis_index("tm"), lax.axis_index("space")
    opening = opening_guess_profile[0]
    rough = rough_decay_factor[0]
    width, rows, depth = opening.shape
    steps, slots = tile_ids.shape
    tile = tile_blocks.shape[-1]
    home, others, rounds = routes(windows, bricks)
    place = jnp.array([home] + others, jnp.int32)
    place = jnp.where(window % 2 == 0, place, bricks - 1 - place)

    rung = rows // SUB
    live = jnp.arange(slots) < tile_count
    per_row = depth // tile
    line = tile_ids // per_row
    part = jnp.where(live, tile_ids % per_row, -1)
    cells = jnp.stack([line // rows * rung + line % rung, line % rows // rung, part, part], axis=-1)
    cells = cells.astype(jnp.float32).reshape(-1, depth)
    list_rows = cells.shape[0]
    cells = jnp.pad(cells, ((0, SUB - cells.shape[0]), (0, 0)))[None]

    def blocked(value):
        return value.reshape(-1, SUB, rung, depth).swapaxes(1, 2).reshape(-1, SUB, depth)

    group = depth // tile
    share = tile // group
    blocks = jnp.concatenate([tile_blocks[:, :, g * share : (g + 1) * share] for g in range(group)], axis=-1)
    blocks = blocks.reshape(-1, SUB, depth)
    early = EARLY * steps // 8
    cut = early * (blocks.shape[0] // steps)
    fields = [blocked(value) for value in (opening, thermal_forcing[0], capacity)]
    pack = jnp.concatenate(fields + [blocks[:cut], cells])
    shape = (bricks, width, rung, depth)

    def spread(value):
        return [lax.ppermute(value, axes, pairs) for pairs in rounds]

    def swap(value):
        return lax.all_to_all(value, "tm", 0, 0, tiled=True)

    packs = [pack] + spread(pack)
    blocks_late = [blocks[cut:]] + spread(blocks[cut:])
    states = run_steps(place, None, packs, None, shape, list_rows, 0, early, slots, tile)
    states = run_steps(place, states, packs, blocks_late, shape, list_rows, early, steps - early, slots, tile)

    held_here = brick == place[0]
    ending = jnp.where(held_here, states[0], 0.0)
    for pairs, state in reversed(list(zip(rounds, states[1:]))):
        ending = ending + lax.ppermute(state, axes, [(b, a) for a, b in pairs])

    ending = ending.reshape(width, rung, SUB, depth).swapaxes(1, 2).reshape(width, rows, depth)
    shift = jnp.where(window == 0, ending, ending - rough * opening)
    parts = jnp.concatenate([shift.reshape(windows, -1, depth), rough.reshape(windows, -1, depth)], axis=1)
    result = swap(recurrence(swap(parts))).reshape(width, rows, depth)
    updated = jnp.where(window == 0, opening, result)
    return (updated[None], ending[None])


def solution(mesh):
    in_specs = (
        P("tm", "space", None, None),
        P("space", None, None),
        P("tm", "space", None, None),
        P("tm", "space", None, None),
        P("tm", "space"),
        P("tm", "space"),
        P("tm", "space", None, None),
    )
    out_specs = (P("tm", "space", None, None), P("tm", "space", None, None))
    return jax.shard_map(shards, mesh=mesh, in_specs=in_specs, out_specs=out_specs, check_vma=False)
```

```python
import functools

import jax
import jax.numpy as jnp
from jax import lax
from jax.experimental import pallas as pl
from jax.experimental.pallas import tpu as pltpu
from jax.sharding import PartitionSpec as P

SWEEPS = 4
COND = 1.0
SUB = 8
LANE = 128
EARLY = 2
SPAN = 4
CHUNKS = 4


def span_of(planes, most):
    return max(n for n in range(1, most + 1) if planes % n == 0)


def steps_kernel(shape, slots, tile, first, steps, own_blocks, *refs):
    bricks, width, rung, depth = shape
    planes, thick = bricks * width, width * rung
    half = depth // LANE
    count = bricks * slots
    share = tile * tile // depth

    def take(n):
        nonlocal refs
        head, refs = refs[:n], refs[n:]
        return head

    (place,) = take(1)
    if own_blocks:
        packs = take(bricks)
        states = [pack.at[pl.ds(0, thick)] for pack in packs]
        blocks = [pack.at[pl.ds(3 * thick, steps * slots * share // SUB)] for pack in packs]
    else:
        states, packs, blocks = take(bricks), take(bricks), take(bricks)
    outs = take(bricks)
    field, other, source, capacity, inverse, rhs, kept, current, picked, fixes, held, raw, whole_lists, lists, load_sem, held_sem, list_sem = refs
    stack = slots * share // SUB

    def fetch_blocks(step, slot):
        return [
            pltpu.make_async_copy(blocks[i].at[pl.ds(step * stack, stack)], held.at[slot, i], held_sem.at[slot, i])
            for i in range(bricks)
        ]

    def slab(i, lead):
        return pl.ds((place[i] * width + lead) * rung, thick)

    loads = []
    for i in range(bricks):
        loads.append((packs[i].at[pl.ds(2 * thick, thick)], capacity.at[slab(i, 0)]))
    for i in range(bricks):
        loads.append((states[i], field.at[slab(i, 1)]))
        loads.append((packs[i].at[pl.ds(thick, thick)], source.at[slab(i, 0)]))
    loads = [pltpu.make_async_copy(*ends, load_sem.at[n]) for n, ends in enumerate(loads)]
    tail = packs[0].shape[0] - 1
    raw_copies = [pltpu.make_async_copy(packs[i].at[tail], raw.at[i], list_sem.at[i]) for i in range(bricks)]
    for copy in raw_copies:
        copy.start()
    for copy in loads:
        copy.start()
    for copy in fetch_blocks(0, 0):
        copy.start()

    zero = jnp.zeros((rung, SUB, depth), jnp.float32)
    for edge in (0, planes + 1):
        field[pl.ds(edge * rung, rung)] = zero
        other[pl.ds(edge * rung, rung)] = zero
    for copy in raw_copies:
        copy.wait()
    whole_lists[...] = raw[:, : whole_lists.shape[1], :].astype(jnp.int32)
    list_copy = pltpu.make_async_copy(whole_lists, lists, list_sem.at[0])
    list_copy.start()
    for copy in loads[:bricks]:
        copy.wait()

    def invert(x, _):
        plane = pl.ds(x * rung, rung)
        inverse[plane] = 1.0 / (capacity[plane] + 6.0 * COND)
        return 0

    lax.fori_loop(0, planes, invert, 0)
    for copy in loads[bricks:]:
        copy.wait()
    list_copy.wait()

    sub = lax.broadcasted_iota(jnp.int32, (SUB, LANE), 0)
    top, bottom = sub == 0, sub == SUB - 1
    line = lax.broadcasted_iota(jnp.int32, (depth, depth), 0)
    column = lax.broadcasted_iota(jnp.int32, (depth, depth), 1)
    beside = jnp.where(jnp.abs(line - column) == 1, 1.0, 0.0).astype(jnp.bfloat16)
    span = span_of(planes, SPAN)
    chunks = span_of(planes // span, CHUNKS)

    def split(value):
        coarse = value.astype(jnp.bfloat16)
        return coarse, (value - coarse.astype(jnp.float32)).astype(jnp.bfloat16)

    def product(value, matrix):
        coarse, fine = split(value)
        return jnp.dot(coarse, matrix, preferred_element_type=jnp.float32) + jnp.dot(
            fine, matrix, preferred_element_type=jnp.float32
        )

    def sweep(src, dst, opening):
        def sides_of(n):
            whole = src[pl.ds((n * span + 1) * rung, span * rung)].reshape(span * rung * SUB, depth)
            return product(whole, beside).reshape(span * rung, SUB, depth)

        def update(n, along):
            base = n * span * rung
            for h in range(half):
                lanes = pl.ds(h * LANE, LANE)

                def line_of(r, lead, tail):
                    return [src[base + q * rung + r, :, lanes] for q in range(lead, span + 2 - tail)]

                above = [jnp.where(top, 0.0, pltpu.roll(v, 1, 0)) for v in line_of(rung - 1, 1, 1)]
                line = line_of(0, 0, 0)
                for r in range(rung):
                    if r + 1 < rung:
                        after = line_of(r + 1, 0, 0)
                        below = after[1:-1]
                    else:
                        after = None
                        below = [jnp.where(bottom, 0.0, pltpu.roll(v, SUB - 1, 0)) for v in line_of(0, 1, 1)]
                    for p in range(span):
                        at = base + p * rung + r
                        total = (line[p] + line[p + 2]) + (above[p] + below[p])
                        total = total + along[p * rung + r, :, h * LANE : (h + 1) * LANE]
                        if opening:
                            start = capacity[at, :, lanes] * line[p + 1] + source[at, :, lanes]
                            rhs[at, :, lanes] = start
                        else:
                            start = rhs[at, :, lanes]
                        dst[at + rung, :, lanes] = (start + COND * total) * inverse[at, :, lanes]
                    above, line = line[1:-1], after

        def batch(m, _):
            along = sides_of(m * chunks)
            for n in range(chunks):
                coming = sides_of(m * chunks + n + 1) if n + 1 < chunks else None
                update(m * chunks + n, along)
                along = coming
            return 0

        lax.fori_loop(0, planes // (span * chunks), batch, 0)

    quarter = lax.broadcasted_iota(jnp.int32, (1, depth), 1) // tile
    group = depth // tile
    gathers = jnp.where(line // tile == (column % tile) // share, 1.0, 0.0).astype(jnp.bfloat16)
    repeats = jnp.where(line % tile == column % tile, 1.0, 0.0).astype(jnp.bfloat16)
    own_line = lax.broadcasted_iota(jnp.int32, (share, depth), 0)
    own_lane = lax.broadcasted_iota(jnp.int32, (share, depth), 1)
    diagonal = own_line == own_lane % share
    tiles = [(i, s) for i in range(bricks) for s in range(slots)]

    def cell_of(step, i, s):
        at = ((first + step) * slots + s) * 4
        spot = [lists[i, (at + k) // depth, (at + k) % depth] for k in range(3)]
        return spot[0] + (place[i] * width + 1) * rung, spot[1], spot[2]

    def one_step(step, _):
        slot = step % 2

        @pl.when(step + 1 < steps)
        def _():
            for copy in fetch_blocks(step + 1, 1 - slot):
                copy.start()

        for n, (i, s) in enumerate(tiles):
            x, u, _unused = cell_of(step, i, s)
            kept[n : n + 1, :] = field[x, pl.ds(u, 1), :]
        sweep(field, other, True)
        for _pair in range((SWEEPS - 2) // 2):
            sweep(other, field, False)
            sweep(field, other, False)
        sweep(other, field, False)

        for n, (i, s) in enumerate(tiles):
            x, u, part = cell_of(step, i, s)
            value = field[x, pl.ds(u, 1), :]
            current[n : n + 1, :] = value
            delta = jnp.where(quarter == part, value - kept[n : n + 1, :], 0.0)
            picked[n : n + 1, :] = delta
        for copy in fetch_blocks(step, slot):
            copy.wait()

        picked[...] = product(picked[...], repeats)
        thin = share // SUB
        terms = []
        for n, (i, s) in enumerate(tiles):
            block = held[slot, i, pl.ds(s * thin, thin)].reshape(share, depth)
            terms.append(block * picked[n : n + 1, :])
        sums = product(jnp.concatenate(terms, axis=0), gathers)
        for n in range(count):
            fix = jnp.where(diagonal, sums[n * share : (n + 1) * share], 0.0)
            fixes[n : n + 1, :] = jnp.sum(fix, axis=0, keepdims=True)

        for n, (i, s) in enumerate(tiles):
            x, u, part = cell_of(step, i, s)
            value = current[n : n + 1, :] + fixes[n : n + 1, :]
            pltpu.store(field.at[x, pl.ds(u, 1), :], value, mask=quarter == part)
        return 0

    lax.fori_loop(0, steps, one_step, 0)
    stores = [
        pltpu.make_async_copy(field.at[slab(i, 1)], outs[i], load_sem.at[i]) for i in range(bricks)
    ]
    for copy in stores:
        copy.start()
    for copy in stores:
        copy.wait()


def run_steps(place, states, packs, blocks, shape, list_rows, first, steps, slots, tile):
    bricks, width, rung, depth = shape
    planes = bricks * width
    count = bricks * slots
    body = functools.partial(steps_kernel, shape, slots, tile, first, steps, blocks is None)
    smem = pl.BlockSpec(memory_space=pltpu.SMEM)
    hbm = pl.BlockSpec(memory_space=pl.ANY)
    operands = list(packs) if blocks is None else list(states) + list(packs) + list(blocks)
    grid_shape = (planes * rung, SUB, depth)
    wide_shape = ((planes + 2) * rung, SUB, depth)
    cells = planes * rung * SUB * depth
    return pl.pallas_call(
        body,
        out_shape=[jax.ShapeDtypeStruct((width * rung, SUB, depth), jnp.float32)] * bricks,
        in_specs=[smem] + [hbm] * len(operands),
        out_specs=[hbm] * bricks,
        scratch_shapes=[
            pltpu.VMEM(wide_shape, jnp.float32),
            pltpu.VMEM(wide_shape, jnp.float32),
            pltpu.VMEM(grid_shape, jnp.float32),
            pltpu.VMEM(grid_shape, jnp.float32),
            pltpu.VMEM(grid_shape, jnp.float32),
            pltpu.VMEM(grid_shape, jnp.float32),
            pltpu.VMEM((count, depth), jnp.float32),
            pltpu.VMEM((count, depth), jnp.float32),
            pltpu.VMEM((count, depth), jnp.float32),
            pltpu.VMEM((count, depth), jnp.float32),
            pltpu.VMEM((2, bricks, slots * tile * tile // depth // SUB, SUB, depth), jnp.float32),
            pltpu.VMEM((bricks, SUB, depth), jnp.float32),
            pltpu.VMEM((bricks, list_rows, depth), jnp.int32),
            pltpu.SMEM((bricks, list_rows, depth), jnp.int32),
            pltpu.SemaphoreType.DMA((3 * bricks,)),
            pltpu.SemaphoreType.DMA((2, bricks)),
            pltpu.SemaphoreType.DMA((bricks,)),
        ],
        compiler_params=pltpu.CompilerParams(vmem_limit_bytes=60 * 1024 * 1024),
        cost_estimate=pl.CostEstimate(
            flops=cells * steps * SWEEPS * 10, bytes_accessed=cells * 4 * steps * 8, transcendentals=0
        ),
    )(place, *operands)


def recurrence(factors, shifts):
    def body(factor, shift, out):
        x = shift[0]
        out[0] = x
        for j in range(1, shifts.shape[0]):
            out[j] = x
            x = factor[j] * x + shift[j]

    return pl.pallas_call(body, out_shape=jax.ShapeDtypeStruct(shifts.shape, jnp.float32))(factors, shifts)


def routes(windows, bricks):
    home = bricks // 2 - 1
    others = [z for z in range(home + 1, bricks)] + [z for z in range(home)]

    def at(t, z):
        return t * bricks + (z if t % 2 == 0 else bricks - 1 - z)

    rounds = [[(at(t, z), at(t, home)) for t in range(windows)] for z in others]
    return home, others, rounds


def shards(
    opening_guess_profile,
    capacity,
    thermal_forcing,
    rough_decay_factor,
    tile_ids,
    tile_count,
    tile_blocks,
):
    axes = ("tm", "space")
    windows, bricks = lax.axis_size("tm"), lax.axis_size("space")
    window, brick = lax.axis_index("tm"), lax.axis_index("space")
    opening = opening_guess_profile[0]
    rough = rough_decay_factor[0]
    width, rows, depth = opening.shape
    steps, slots = tile_ids.shape
    tile = tile_blocks.shape[-1]
    home, others, rounds = routes(windows, bricks)
    place = jnp.array([home] + others, jnp.int32)
    place = jnp.where(window % 2 == 0, place, bricks - 1 - place)

    rung = rows // SUB
    live = jnp.arange(slots) < tile_count
    per_row = depth // tile
    line = tile_ids // per_row
    part = jnp.where(live, tile_ids % per_row, -1)
    cells = jnp.stack([line // rows * rung + line % rung, line % rows // rung, part, part], axis=-1)
    cells = cells.astype(jnp.float32).reshape(-1, depth)
    list_rows = cells.shape[0]
    cells = jnp.pad(cells, ((0, SUB - cells.shape[0]), (0, 0)))[None]

    def blocked(value):
        return value.reshape(-1, SUB, rung, depth).swapaxes(1, 2).reshape(-1, SUB, depth)

    group = depth // tile
    share = tile // group
    blocks = jnp.concatenate([tile_blocks[:, :, g * share : (g + 1) * share] for g in range(group)], axis=-1)
    blocks = blocks.reshape(-1, SUB, depth)
    early = EARLY * steps // 8
    cut = early * (blocks.shape[0] // steps)
    fields = [blocked(value) for value in (opening, thermal_forcing[0], capacity)]
    pack = jnp.concatenate(fields + [blocks[:cut], cells])
    shape = (bricks, width, rung, depth)

    def spread(value):
        return [lax.ppermute(value, axes, pairs) for pairs in rounds]

    def swap(value):
        return lax.all_to_all(value, "tm", 0, 0, tiled=True)

    packs = [pack] + spread(pack)
    blocks_late = [blocks[cut:]] + spread(blocks[cut:])
    states = run_steps(place, None, packs, None, shape, list_rows, 0, early, slots, tile)
    states = run_steps(place, states, packs, blocks_late, shape, list_rows, early, steps - early, slots, tile)

    factors = swap((rough + states[0][0, 0, 0] * 0.0).reshape(windows, -1, depth))
    held_here = brick == place[0]
    ending = jnp.where(held_here, states[0], 0.0)
    for pairs, state in reversed(list(zip(rounds, states[1:]))):
        ending = ending + lax.ppermute(state, axes, [(b, a) for a, b in pairs])

    ending = ending.reshape(width, rung, SUB, depth).swapaxes(1, 2).reshape(width, rows, depth)
    shift = jnp.where(window == 0, ending, ending - rough * opening)
    result = swap(recurrence(factors, swap(shift.reshape(windows, -1, depth)))).reshape(width, rows, depth)
    updated = jnp.where(window == 0, opening, result)
    return (updated[None], ending[None])


def solution(mesh):
    in_specs = (
        P("tm", "space", None, None),
        P("space", None, None),
        P("tm", "space", None, None),
        P("tm", "space", None, None),
        P("tm", "space"),
        P("tm", "space"),
        P("tm", "space", None, None),
    )
    out_specs = (P("tm", "space", None, None), P("tm", "space", None, None))
    return jax.shard_map(shards, mesh=mesh, in_specs=in_specs, out_specs=out_specs, check_vma=False)
```
